128 devices in a mesh: row: 8 (over y_lo, x), col: 16 (over z, y_hi, core).
Axes of the slice: x: 4, y: 4 (y_hi: 2, y_lo: 2; y = y_hi * 2 + y_lo), z: 4, core: 2. Of those that a mesh axis runs over, the one named last changes fastest.
Arguments:
- history: bfloat16 [2, 8192, 8192], P(None, 'row', 'col'), may hold values from -2 to 2, as said below
- start_strip: float32 [2, 2048, 8192], P(None, 'col', 'row'), may hold values from -6 to 6
- coupling: float32 [32], replicated, may hold values from 0.5 to 1.5
- dyson_inverse: float32 [2, 2, 64, 64], replicated, may hold values from -3 to 3, as said below
Outputs:
- earlier: float32 [2, 2048, 8192], P(None, None, 'col')
- later: float32 [2, 2048, 8192], P(None, 'col', 'row')
The draws below stay inside these ranges and needn't reach their ends.
Inputs may be any that keep to these rules, and one draw needn't show every extreme that they name: history is anti-Hermitian: its element at row (s, a), column (t, b) is minus the complex conjugate of its element at row (t, b), column (s, a). `dyson_inverse`: each group's inverse is lower triangular in time.
All inputs are finite; a program needn't handle non-finite values.
Results may differ from the reference program's by a relative error of at most 0.0043.
Values may be sent and summed in bfloat16 or wider, within the bound.
No kernel may reach another device: no remote copies, remote signals or barrier semaphores. Data moves between devices by JAX's collectives and lax.ppermute only.
A program may use at most 192 MiB of HBM per device.

```python
import math
import jax
import jax.numpy as jnp
from jax import lax

NO = 32
C = 64
NT = 256


def draw_history(key, part):
    width = NT * NO
    key_real = jax.random.fold_in(key, 11)
    key_imag = jax.random.fold_in(key, 12)
    noise_real = jax.random.normal(key_real, (width, width), jnp.float32) * width ** (-0.5)
    noise_imag = jax.random.normal(key_imag, (width, width), jnp.float32) * width ** (-0.5)
    real_part = (noise_real - noise_real.T) * 0.5
    imag_part = (noise_imag + noise_imag.T) * 0.5
    return jnp.stack([real_part, imag_part]).astype(jnp.bfloat16)


def draw_dyson_inverse(key, part):
    key_real = jax.random.fold_in(key, 21)
    key_imag = jax.random.fold_in(key, 22)
    lower = jnp.tril(jnp.ones((C, C), jnp.float32))
    noise_real = jax.random.normal(key_real, (2, C, C), jnp.float32) * (0.5 * C ** (-0.5))
    noise_imag = jax.random.normal(key_imag, (2, C, C), jnp.float32) * (0.5 * C ** (-0.5))
    real_part = jnp.eye(C, dtype=jnp.float32)[None] + noise_real * lower[None]
    imag_part = noise_imag * lower[None]
    return jnp.stack([real_part, imag_part], axis=1)


def levels(own_key, dims, shards, least, high):
    level = 1.0
    for axis_at, blocks in shards:
        steps = jax.random.uniform(jax.random.fold_in(jax.random.fold_in(own_key, 6), axis_at), (blocks,), jnp.float32, least / len(shards), high / len(shards))
        level = level * jnp.repeat(jnp.exp(steps), dims[axis_at] // blocks).reshape((-1,) + (1,) * (len(dims) - 1 - axis_at))
    return level


def normal_values(own_key, dims, scale, limit, shards=(), kind=jnp.bfloat16):
    loudness = levels(own_key, dims, shards, -0.22, 0.18) if shards else 1.0
    array = jax.random.normal(own_key, dims, jnp.float32) * scale * loudness
    return jnp.minimum(jnp.maximum(array, -limit), limit).astype(kind)


def setup_inputs(seed: int = 0) -> dict:
    splits = jax.random.split(jax.random.key(seed), 5)
    history = draw_history(jax.random.fold_in(splits[4], 71), 0)
    start_strip = normal_values(splits[1], (2, C * NO, NT * NO), 1.0, 6.0, ((1, 16), (2, 8)), jnp.float32)
    coupling = jnp.clip(jnp.exp(jax.random.uniform(splits[2], (NO,), jnp.float32, math.log(0.5), math.log(1.5))), 0.5, 1.5)
    dyson_inverse = draw_dyson_inverse(jax.random.fold_in(splits[4], 71), 0)
    return {"history": history, "start_strip": start_strip, "coupling": coupling, "dyson_inverse": dyson_inverse}


TIME_STEP = 0.15


def complex_product(first_pair, second_pair):
    real_out = jnp.dot(first_pair[0], second_pair[0], precision=lax.Precision.HIGHEST, preferred_element_type=jnp.float32) - jnp.dot(first_pair[1], second_pair[1], precision=lax.Precision.HIGHEST, preferred_element_type=jnp.float32)
    imag_out = jnp.dot(first_pair[0], second_pair[1], precision=lax.Precision.HIGHEST, preferred_element_type=jnp.float32) + jnp.dot(first_pair[1], second_pair[0], precision=lax.Precision.HIGHEST, preferred_element_type=jnp.float32)
    return jnp.stack([real_out, imag_out])


def self_energy(green, row_weight, col_weight):
    magnitude = green[0] * green[0] + green[1] * green[1]
    factor = -(row_weight[:, None] * col_weight[None, :]) * magnitude
    return green * factor[None]


def dyson_apply(inverse, source):
    group_len = inverse.shape[1]
    flat_width = source.shape[1] * source.shape[2] // group_len
    flat = source.reshape(2, group_len, flat_width)
    real_out = jnp.dot(inverse[0], flat[0], precision=lax.Precision.HIGHEST, preferred_element_type=jnp.float32) - jnp.dot(inverse[1], flat[1], precision=lax.Precision.HIGHEST, preferred_element_type=jnp.float32)
    imag_out = jnp.dot(inverse[0], flat[1], precision=lax.Precision.HIGHEST, preferred_element_type=jnp.float32) + jnp.dot(inverse[1], flat[0], precision=lax.Precision.HIGHEST, preferred_element_type=jnp.float32)
    return jnp.stack([real_out, imag_out]).reshape(source.shape)


def reference(history, start_strip, coupling, dyson_inverse):
    hist_wide = history.astype(jnp.float32)
    row_weight = jnp.tile(coupling, C)
    col_weight = jnp.tile(coupling, NT)
    sigma_first = self_energy(start_strip, row_weight, col_weight).astype(jnp.bfloat16)
    sigma_first = lax.optimization_barrier(sigma_first).astype(jnp.float32)
    earlier = dyson_apply(dyson_inverse[0], TIME_STEP * complex_product(sigma_first, hist_wide))
    sigma_second = self_energy(earlier, row_weight, col_weight).astype(jnp.bfloat16)
    sigma_second = lax.optimization_barrier(sigma_second).astype(jnp.float32)
    later = dyson_apply(dyson_inverse[1], TIME_STEP * complex_product(sigma_second, hist_wide))
    return earlier, later
```

```python
import functools

import jax
import jax.numpy as jnp
from jax import lax
from jax.experimental import pallas as pl
from jax.experimental.pallas import tpu as pltpu
from jax.sharding import Mesh
from jax.sharding import PartitionSpec as P

AXES = ("yl", "x", "z", "yh", "core")
SIZES = (2, 4, 4, 2, 2)
ROW = ("yl", "x")
COL = ("z", "yh", "core")
TIME_STEP = 0.15
CHUNKS = 2
LANES = 128
BF16 = jnp.bfloat16
F32 = jnp.float32
HIGHEST = lax.Precision.HIGHEST


def coordinates(flat):
    found = []
    for size in reversed(SIZES):
        found.append(flat % size)
        flat //= size
    return dict(zip(AXES, reversed(found)))


def flat_index(where):
    flat = 0
    for name, size in zip(AXES, SIZES):
        flat = flat * size + where[name]
    return flat


def pairs(change):
    devices = 1
    for size in SIZES:
        devices *= size
    out = []
    for device in range(devices):
        where = coordinates(device)
        out.append((device, flat_index({**where, **change(where)})))
    return out


def ring_pairs(ring, second):
    return pairs(lambda w: {ring: w[ring] ^ (3 if (w["core"] == 1) != second else 1)})


ROW_STEPS = (
    pairs(lambda w: {"yl": w["yl"] ^ 1}),
    ring_pairs("x", False),
    ring_pairs("x", True),
)
COL_STEPS = (
    pairs(lambda w: {"yh": w["yh"] ^ 1}),
    ring_pairs("z", False),
    ring_pairs("z", True),
)
CORE_STEP = pairs(lambda w: {"core": w["core"] ^ 1})


def send(value, step):
    return lax.ppermute(value, AXES, step)


def place_of(low, ring, core):
    first = (ring ^ (ring >> 1)) & 1
    second = ring >> 1
    swap = core == 1
    return low + 2 * jnp.where(swap, second, first) + 4 * jnp.where(swap, first, second)


def ring_group(place, core):
    low = place & 1
    one = (place >> 1) & 1
    two = (place >> 2) & 1
    swap = core == 1
    first = jnp.where(swap, two, one)
    second = jnp.where(swap, one, two)
    return 2 * (2 * second + (first ^ second)) + low


def gather_steps(block, steps):
    held = block
    for step in steps[:2]:
        held = jnp.concatenate([held, send(held, step)], axis=0)
    return held, send(held, steps[2])


def arrange_body(scalars, own_ref, other_ref, near_ref, far_ref):
    own_near = scalars[2] == 1

    @pl.when(own_near)
    def _():
        near_ref[...] = own_ref[...]
        far_ref[...] = other_ref[...]

    @pl.when(jnp.logical_not(own_near))
    def _():
        near_ref[...] = other_ref[...]
        far_ref[...] = own_ref[...]


def arrange_history(scalars, own, other):
    depth, width = own.shape[1:]
    spec_in = pl.BlockSpec((2, depth, LANES), lambda j, s: (0, 0, s[0] ^ j))
    spec_out = pl.BlockSpec((2, depth, LANES), lambda j, s: (0, 0, j))
    return pl.pallas_call(
        arrange_body,
        out_shape=[jax.ShapeDtypeStruct(own.shape, BF16)] * 2,
        grid_spec=pltpu.PrefetchScalarGridSpec(
            num_scalar_prefetch=1,
            grid=(width // LANES,),
            in_specs=[spec_in, spec_in],
            out_specs=[spec_out, spec_out],
        ),
        compiler_params=pltpu.CompilerParams(vmem_limit_bytes=24 << 20),
        cost_estimate=pl.CostEstimate(flops=0, bytes_accessed=8 << 20, transcendentals=0),
        name="arrange_history",
    )(scalars, own, other)


def first_body(low_ref, high_ref, hist_ref, out_ref, left):
    blocks, _, rows, depth = low_ref.shape
    half = blocks * rows
    full = 2 * half

    @pl.when(pl.program_id(0) == 0)
    def _():
        for at, ref in ((0, low_ref), (half, high_ref)):
            for b in range(blocks):
                real = ref[b, 0]
                imag = ref[b, 1]
                top = pl.ds(at + b * rows, rows)
                bottom = pl.ds(full + at + b * rows, rows)
                left[top, :depth] = real
                left[top, depth:] = -imag
                left[bottom, :depth] = imag
                left[bottom, depth:] = real

    out = jnp.dot(left[:, :depth], hist_ref[0], preferred_element_type=F32)
    out += jnp.dot(left[:, depth:], hist_ref[1], preferred_element_type=F32)
    out_ref[0] = out[:full].astype(out_ref.dtype)
    out_ref[1] = out[full:].astype(out_ref.dtype)


def first_product(low, high, hist, kind):
    blocks, _, rows, depth = low.shape
    full = 2 * blocks * rows
    width = hist.shape[2]
    tile = 256
    whole = pl.BlockSpec(low.shape, lambda t: (0, 0, 0, 0))
    return pl.pallas_call(
        first_body,
        out_shape=jax.ShapeDtypeStruct((2, full, width), kind),
        grid=(width // tile,),
        in_specs=[whole, whole, pl.BlockSpec((2, depth, tile), lambda t: (0, 0, t))],
        out_specs=pl.BlockSpec((2, full, tile), lambda t: (0, 0, t)),
        scratch_shapes=[pltpu.VMEM((2 * full, 2 * depth), BF16)],
        compiler_params=pltpu.CompilerParams(vmem_limit_bytes=40 << 20),
        cost_estimate=pl.CostEstimate(
            flops=8 * full * depth * width, bytes_accessed=8 << 20, transcendentals=0
        ),
        name="first_product",
    )(low, high, hist)


def middle_body(keep_ref, one_ref, two_ref, three_ref, solve_ref, next_ref, weight_ref, earlier_ref, sigma_ref):
    rows = three_ref.shape[1]
    parts = []
    for c in range(2):
        total = keep_ref[c] + one_ref[c].astype(F32) + two_ref[c].astype(F32) + three_ref[c].astype(F32)
        parts.append(TIME_STEP * total)
    source = jnp.concatenate(parts, axis=0)
    green = jnp.dot(solve_ref[...], source, precision=HIGHEST, preferred_element_type=F32)
    real = green[:rows]
    imag = green[rows:]
    earlier_ref[0, 0] = real.astype(BF16)
    earlier_ref[0, 1] = imag.astype(BF16)
    factor = weight_ref[...] * (real * real + imag * imag)
    sigma = jnp.concatenate([real * factor, imag * factor], axis=0)
    mixed = jnp.dot(next_ref[...], sigma, precision=HIGHEST, preferred_element_type=F32)
    sigma_ref[0, 0] = mixed[:rows].astype(BF16)
    sigma_ref[0, 1] = mixed[rows:].astype(BF16)


def middle(keep, one, two, three, solve, following, weight):
    rows = three.shape[1]
    strip = pl.BlockSpec((2, rows, LANES), lambda i: (0, 0, 0))
    square = pl.BlockSpec((2 * rows, 2 * rows), lambda i: (0, 0))
    share = pl.BlockSpec((1, 2, rows, LANES), lambda i: (0, 0, 0, 0))
    return pl.pallas_call(
        middle_body,
        out_shape=[jax.ShapeDtypeStruct((1, 2, rows, LANES), BF16)] * 2,
        grid=(1,),
        in_specs=[strip] * 4 + [square] * 2 + [pl.BlockSpec((rows, LANES), lambda i: (0, 0))],
        out_specs=[share, share],
        compiler_params=pltpu.CompilerParams(vmem_limit_bytes=40 << 20),
        cost_estimate=pl.CostEstimate(
            flops=12 * 8 * rows * rows * LANES, bytes_accessed=10 << 20, transcendentals=0
        ),
        name="middle",
    )(keep, one, two, three, solve, following, weight)


def second_body(start, count, low_ref, high_ref, near_ref, far_ref, out_ref, left):
    blocks = low_ref.shape[0]
    span = blocks * LANES
    depth = 2 * span

    @pl.when(pl.program_id(0) == 0)
    def _():
        for at, ref in ((0, low_ref), (span, high_ref)):
            for b in range(blocks):
                real = ref[b, 0, start : start + count, :]
                imag = ref[b, 1, start : start + count, :]
                here = pl.ds(at + b * LANES, LANES)
                there = pl.ds(depth + at + b * LANES, LANES)
                left[:count, here] = -real
                left[:count, there] = -imag
                left[count:, here] = -imag
                left[count:, there] = real

    def term(at, tile):
        return lax.dot_general(
            left[:, at : at + span], tile, (((1,), (1,)), ((), ())), preferred_element_type=F32
        )

    out = term(0, near_ref[0]) + term(span, far_ref[0])
    out += term(depth, near_ref[1]) + term(depth + span, far_ref[1])
    out_ref[0] = out[:count].astype(out_ref.dtype)
    out_ref[1] = out[count:].astype(out_ref.dtype)


def second_product(low, high, near, far, start, count, kind):
    depth, width = near.shape[1:]
    tile = 256
    whole = pl.BlockSpec(low.shape, lambda s: (0, 0, 0, 0))
    strip = pl.BlockSpec((2, tile, width), lambda s: (0, s, 0))
    return pl.pallas_call(
        functools.partial(second_body, start, count),
        out_shape=jax.ShapeDtypeStruct((2, count, depth), kind),
        grid=(depth // tile,),
        in_specs=[whole, whole, strip, strip],
        out_specs=pl.BlockSpec((2, count, tile), lambda s: (0, 0, s)),
        scratch_shapes=[pltpu.VMEM((2 * count, 4 * width), BF16)],
        compiler_params=pltpu.CompilerParams(vmem_limit_bytes=40 << 20),
        cost_estimate=pl.CostEstimate(
            flops=16 * count * width * depth, bytes_accessed=8 << 20, transcendentals=0
        ),
        name="second_product",
    )(low, high, near, far)


def assemble_body(scalars, *refs):
    out_ref = refs[-1]
    half = len(refs) // 2
    times, orbitals = out_ref.shape[1:3]
    width = orbitals // 2
    core = scalars[3]
    for at, group in ((core, refs[:half]), (1 - core, refs[half:-1])):
        per_chunk = width // half
        for k, ref in enumerate(group):
            for c in range(2):
                value = ref[0, c].astype(F32).reshape(times, per_chunk, LANES)
                row = pl.multiple_of(at * width + k * per_chunk, 8)
                out_ref[c, :, pl.ds(row, per_chunk), :] = value


def assemble_earlier(scalars, mine, others, times, orbitals):
    rows = mine[0].shape[2]
    blocks = mine[0].shape[0]
    own = pl.BlockSpec((1, 2, rows, LANES), lambda j, s: (s[0] ^ j, 0, 0, 0))
    other = pl.BlockSpec((1, 2, rows, LANES), lambda j, s: (s[1] ^ j, 0, 0, 0))
    return pl.pallas_call(
        assemble_body,
        out_shape=jax.ShapeDtypeStruct((2, times, orbitals, blocks * LANES), F32),
        grid_spec=pltpu.PrefetchScalarGridSpec(
            num_scalar_prefetch=1,
            grid=(blocks,),
            in_specs=[own] * len(mine) + [other] * len(others),
            out_specs=pl.BlockSpec((2, times, orbitals, LANES), lambda j, s: (0, 0, 0, j)),
        ),
        compiler_params=pltpu.CompilerParams(vmem_limit_bytes=40 << 20),
        cost_estimate=pl.CostEstimate(flops=0, bytes_accessed=12 << 20, transcendentals=0),
        name="assemble_earlier",
    )(scalars, *mine, *others)


def one_hot(position, count):
    return (position[:, None] == jnp.arange(count, dtype=jnp.int32)[None, :]).astype(F32)


def exact_dot(left, right):
    return jnp.dot(left, right, precision=HIGHEST, preferred_element_type=F32)


def spread(inverse, row_time, col_time, orbitals):
    times = inverse.shape[1]
    pick_row = one_hot(row_time, times)
    pick_col = one_hot(col_time, times)
    at = jnp.arange(row_time.shape[0], dtype=jnp.int32) % orbitals
    same = (at[:, None] == at[None, :]).astype(F32)
    real, imag = [exact_dot(exact_dot(pick_row, inverse[c]), pick_col.T) * same for c in range(2)]
    return jnp.concatenate(
        [jnp.concatenate([real, -imag], axis=1), jnp.concatenate([imag, real], axis=1)], axis=0
    )


def shards(history, start_strip, coupling, dyson_inverse):
    orbitals = coupling.shape[0]
    times = dyson_inverse.shape[2]
    yl, x, z, yh, core = [lax.axis_index(a) for a in AXES]
    strip_rows, strip_cols = start_strip.shape[1:]
    own_times = strip_rows // orbitals
    half = orbitals // 2
    per_chunk = half // CHUNKS
    chip_times = 2 * own_times
    block_rows = chip_times * per_chunk
    rows = times * per_chunk
    tile_cols = history.shape[2]

    row_place = place_of(yl, x, core)
    other_row_place = place_of(yl, x, 1 - core)
    col_place = place_of(yh, z, core)
    own_near = (row_place >> 2) == core
    other_near = (other_row_place >> 2) == (1 - core)
    scalars = jnp.stack(
        [row_place & 3, other_row_place & 3, own_near.astype(jnp.int32), core]
    ).astype(jnp.int32)

    other_history = send(history, CORE_STEP)
    strip = start_strip.reshape(2, own_times, orbitals, strip_cols)
    col_weight = exact_dot(one_hot(jnp.arange(LANES, dtype=jnp.int32) % orbitals, orbitals), coupling)
    strip_weight = jnp.tile(col_weight, strip_cols // LANES)
    magnitude = strip[0] * strip[0] + strip[1] * strip[1]
    factor = -(coupling[None, :, None] * strip_weight[None, None, :]) * magnitude
    sigma_first = (strip * factor[None]).astype(BF16)
    sigma_own = lax.dynamic_slice_in_dim(sigma_first, half * core, half, axis=2)
    sigma_other = lax.dynamic_slice_in_dim(sigma_first, half * (1 - core), half, axis=2)
    sigma_chip = jnp.concatenate([sigma_own, send(sigma_other, CORE_STEP)], axis=1)

    near, far = arrange_history(scalars, history, other_history)

    block = jnp.arange(8, dtype=jnp.int32)
    group = ring_group(col_place ^ block, core)
    inner = (jnp.arange(chip_times, dtype=jnp.int32) + own_times * core) % chip_times
    time_order = (chip_times * group[:, None] + inner[None, :]).reshape(-1)
    plain_rows = jnp.repeat(jnp.arange(times, dtype=jnp.int32), per_chunk)
    moved_rows = jnp.repeat(time_order, per_chunk)
    solve = spread(dyson_inverse[0], plain_rows, moved_rows, per_chunk)
    following = spread(dyson_inverse[1], moved_rows, plain_rows, per_chunk)

    own_parts = []
    sent_parts = []
    mine = []
    others = []
    for k in range(CHUNKS):
        with jax.named_scope("chunk"):
            piece = sigma_chip[:, :, k * per_chunk : (k + 1) * per_chunk]
            low, high = gather_steps(piece.reshape(1, 2, block_rows, strip_cols), COL_STEPS)
            away = first_product(low, high, far, BF16)
            one = send(away, ROW_STEPS[2])
            keep = first_product(low, high, near, F32)
            width = tile_cols // 2
            two_out = (keep[:, :, width:] + one[:, :, width:].astype(F32)).astype(BF16)
            two = send(two_out, ROW_STEPS[1])
            span = slice(LANES, 2 * LANES)
            three_out = keep[:, :, span] + one[:, :, span].astype(F32) + two[:, :, span].astype(F32)
            three = send(three_out.astype(BF16), ROW_STEPS[0])
            own_row = half * core + k * per_chunk + jnp.arange(rows, dtype=jnp.int32) % per_chunk
            row_weight = exact_dot(one_hot(own_row, orbitals), coupling)
            weight = -(row_weight[:, None] * col_weight[None, :])
            earlier_share, sigma_share = middle(keep, one, two, three, solve, following, weight)

            low, high = gather_steps(sigma_share, ROW_STEPS)
            away = second_product(low, high, near, far, rows // 2, rows // 2, BF16)
            one = send(away, COL_STEPS[2])
            keep = second_product(low, high, near, far, 0, rows // 2, F32)
            size = rows // 4
            two_out = (keep[:, size:] + one[:, size:].astype(F32)).astype(BF16)
            two = send(two_out, COL_STEPS[1])
            span = slice(block_rows, 2 * block_rows)
            three_out = keep[:, span] + one[:, span].astype(F32) + two[:, span].astype(F32)
            three = send(three_out.astype(BF16), COL_STEPS[0])
            span = slice(0, block_rows)
            total = keep[:, span] + one[:, span].astype(F32) + two[:, span].astype(F32) + three.astype(F32)
            total = (TIME_STEP * total).reshape(2, chip_times, per_chunk, strip_cols)
            own_parts.append(total[:, :own_times])
            sent_parts.append(send(total[:, own_times:], CORE_STEP))

            earlier_share, _ = lax.optimization_barrier((earlier_share, high))
            low, high = gather_steps(earlier_share, ROW_STEPS)
            mine.append(jnp.where(own_near, low, high))
            others.append(send(jnp.where(own_near, high, low), CORE_STEP))

    earlier = assemble_earlier(scalars, mine, others, times, orbitals)
    own = jnp.concatenate(own_parts, axis=2)
    arrived = jnp.concatenate(sent_parts, axis=2)
    later = jnp.concatenate(
        [jnp.where(core == 0, own, arrived), jnp.where(core == 0, arrived, own)], axis=2
    )
    return (
        earlier.reshape(2, times * orbitals, tile_cols),
        later.reshape(2, strip_rows, strip_cols),
    )


def solution(mesh):
    finer = Mesh(mesh.devices.reshape(SIZES), AXES)
    in_specs = (P(None, ROW, COL), P(None, COL, ROW), P(), P())
    out_specs = (P(None, None, COL), P(None, COL, ROW))
    return jax.shard_map(
        shards, mesh=finer, in_specs=in_specs, out_specs=out_specs, check_vma=False
    )
```

```python
import functools

import jax
import jax.numpy as jnp
from jax import lax
from jax.experimental import pallas as pl
from jax.experimental.pallas import tpu as pltpu
from jax.sharding import Mesh
from jax.sharding import PartitionSpec as P

AXES = ("yl", "x", "z", "yh", "core")
SIZES = (2, 4, 4, 2, 2)
ROW = ("yl", "x")
COL = ("z", "yh", "core")
TIME_STEP = 0.15
CHUNKS = 2
LANES = 128
BF16 = jnp.bfloat16
F32 = jnp.float32
HIGHEST = lax.Precision.HIGHEST


def coordinates(flat):
    found = []
    for size in reversed(SIZES):
        found.append(flat % size)
        flat //= size
    return dict(zip(AXES, reversed(found)))


def flat_index(where):
    flat = 0
    for name, size in zip(AXES, SIZES):
        flat = flat * size + where[name]
    return flat


def pairs(change):
    devices = 1
    for size in SIZES:
        devices *= size
    out = []
    for device in range(devices):
        where = coordinates(device)
        out.append((device, flat_index({**where, **change(where)})))
    return out


def ring_pairs(ring, second):
    return pairs(lambda w: {ring: w[ring] ^ (3 if (w["core"] == 1) != second else 1)})


ROW_STEPS = (
    pairs(lambda w: {"yl": w["yl"] ^ 1}),
    ring_pairs("x", False),
    ring_pairs("x", True),
)
COL_STEPS = (
    pairs(lambda w: {"yh": w["yh"] ^ 1}),
    ring_pairs("z", False),
    ring_pairs("z", True),
)
CORE_STEP = pairs(lambda w: {"core": w["core"] ^ 1})
COL_ACROSS_IN = pairs(lambda w: {"core": w["core"] ^ 1, "yh": w["yh"] ^ 1})
COL_ACROSS_OUT = COL_ACROSS_IN


def send(value, step):
    return lax.ppermute(value, AXES, step)


def place_of(low, ring, core):
    first = (ring ^ (ring >> 1)) & 1
    second = ring >> 1
    swap = core == 1
    return low + 2 * jnp.where(swap, second, first) + 4 * jnp.where(swap, first, second)


def ring_group(place, core):
    low = place & 1
    one = (place >> 1) & 1
    two = (place >> 2) & 1
    swap = core == 1
    first = jnp.where(swap, two, one)
    second = jnp.where(swap, one, two)
    return 2 * (2 * second + (first ^ second)) + low


def gather_steps(block, steps):
    held = block
    for step in steps[:2]:
        held = jnp.concatenate([held, send(held, step)], axis=0)
    return held, send(held, steps[2])


def arrange_body(scalars, own_ref, other_ref, near_ref, far_ref):
    own_near = scalars[2] == 1

    @pl.when(own_near)
    def _():
        near_ref[...] = own_ref[...]
        far_ref[...] = other_ref[...]

    @pl.when(jnp.logical_not(own_near))
    def _():
        near_ref[...] = other_ref[...]
        far_ref[...] = own_ref[...]


def arrange_history(scalars, own, other):
    depth, width = own.shape[1:]
    spec_in = pl.BlockSpec((2, depth, LANES), lambda j, s: (0, 0, s[0] ^ j))
    spec_out = pl.BlockSpec((2, depth, LANES), lambda j, s: (0, 0, j))
    return pl.pallas_call(
        arrange_body,
        out_shape=[jax.ShapeDtypeStruct(own.shape, BF16)] * 2,
        grid_spec=pltpu.PrefetchScalarGridSpec(
            num_scalar_prefetch=1,
            grid=(width // LANES,),
            in_specs=[spec_in, spec_in],
            out_specs=[spec_out, spec_out],
        ),
        compiler_params=pltpu.CompilerParams(vmem_limit_bytes=24 << 20),
        cost_estimate=pl.CostEstimate(flops=0, bytes_accessed=8 << 20, transcendentals=0),
        name="arrange_history",
    )(scalars, own, other)


def first_body(low_ref, high_ref, hist_ref, out_ref, left):
    blocks, _, rows, depth = low_ref.shape
    half = blocks * rows
    full = 2 * half

    @pl.when(pl.program_id(0) == 0)
    def _():
        for at, ref in ((0, low_ref), (half, high_ref)):
            for b in range(blocks):
                real = ref[b, 0]
                imag = ref[b, 1]
                top = pl.ds(at + b * rows, rows)
                bottom = pl.ds(full + at + b * rows, rows)
                left[top, :depth] = real
                left[top, depth:] = -imag
                left[bottom, :depth] = imag
                left[bottom, depth:] = real

    out = jnp.dot(left[:, :depth], hist_ref[0], preferred_element_type=F32)
    out += jnp.dot(left[:, depth:], hist_ref[1], preferred_element_type=F32)
    out_ref[0] = out[:full].astype(out_ref.dtype)
    out_ref[1] = out[full:].astype(out_ref.dtype)


def first_product(low, high, hist, kind):
    blocks, _, rows, depth = low.shape
    full = 2 * blocks * rows
    width = hist.shape[2]
    tile = 256
    whole = pl.BlockSpec(low.shape, lambda t: (0, 0, 0, 0))
    return pl.pallas_call(
        first_body,
        out_shape=jax.ShapeDtypeStruct((2, full, width), kind),
        grid=(width // tile,),
        in_specs=[whole, whole, pl.BlockSpec((2, depth, tile), lambda t: (0, 0, t))],
        out_specs=pl.BlockSpec((2, full, tile), lambda t: (0, 0, t)),
        scratch_shapes=[pltpu.VMEM((2 * full, 2 * depth), BF16)],
        compiler_params=pltpu.CompilerParams(vmem_limit_bytes=40 << 20),
        cost_estimate=pl.CostEstimate(
            flops=8 * full * depth * width, bytes_accessed=8 << 20, transcendentals=0
        ),
        name="first_product",
    )(low, high, hist)


def lane_weights(coupling, shape, axis):
    orbitals = coupling.shape[0]
    at = lax.rem(lax.broadcasted_iota(jnp.int32, shape, axis), orbitals)
    weights = jnp.zeros(shape, F32)
    for a in range(orbitals):
        weights = jnp.where(at == a, coupling[a], weights)
    return weights


def sigma_body(scalars, coupling, strip_ref, own_ref, other_ref):
    _, own_times, orbitals, width = strip_ref.shape
    half = orbitals // 2
    core = scalars[3]
    col = lane_weights(coupling, (1, LANES), 1)
    col = jnp.concatenate([col] * (width // LANES), axis=1)
    row = lane_weights(coupling, (orbitals, LANES), 0)
    row = jnp.concatenate([row] * (width // LANES), axis=1)
    weight = row * col
    for n in range(own_times):
        real = strip_ref[0, n]
        imag = strip_ref[1, n]
        factor = -weight * (real * real + imag * imag)
        for c, part in ((0, real), (1, imag)):
            sigma = (part * factor).astype(BF16)
            first, second = sigma[:half], sigma[half:]
            own_ref[c, n] = jnp.where(core == 0, first, second)
            other_ref[c, n] = jnp.where(core == 0, second, first)


def sigma_strip(scalars, coupling, strip):
    _, own_times, orbitals, width = strip.shape
    out = jax.ShapeDtypeStruct((2, own_times, orbitals // 2, width), BF16)
    return pl.pallas_call(
        sigma_body,
        out_shape=[out, out],
        in_specs=[
            pl.BlockSpec(memory_space=pltpu.SMEM),
            pl.BlockSpec(memory_space=pltpu.SMEM),
            pl.BlockSpec(memory_space=pltpu.VMEM),
        ],
        out_specs=[pl.BlockSpec(memory_space=pltpu.VMEM)] * 2,
        compiler_params=pltpu.CompilerParams(vmem_limit_bytes=24 << 20),
        cost_estimate=pl.CostEstimate(flops=3 << 20, bytes_accessed=3 << 20, transcendentals=0),
        name="sigma_strip",
    )(scalars, coupling, strip)


def middle_body(
    first_orbital, scalars, coupling, keep_ref, one_ref, two_ref, three_ref, solve_ref, next_ref, earlier_ref, sigma_ref, turn
):
    rows = three_ref.shape[1]
    times = solve_ref.shape[0] // 2
    count = rows // times
    orbitals = coupling.shape[0]
    for c in range(2):
        total = keep_ref[c] + one_ref[c].astype(F32) + two_ref[c].astype(F32) + three_ref[c].astype(F32)
        turn[c] = TIME_STEP * total

    def column(a):
        return jnp.concatenate([turn[c, pl.ds(a, times, stride=count), :] for c in range(2)], axis=0)

    source = jnp.concatenate([column(a) for a in range(count)], axis=1)
    green = jnp.dot(solve_ref[...], source, precision=HIGHEST, preferred_element_type=F32)
    col = lane_weights(coupling, (1, LANES), 1)
    base = scalars[3] * (orbitals // 2) + first_orbital
    weight = jnp.concatenate([-(coupling[base + a] * col) for a in range(count)], axis=1)
    real = green[:times]
    imag = green[times:]
    factor = weight * (real * real + imag * imag)
    sigma = jnp.concatenate([real * factor, imag * factor], axis=0)
    mixed = jnp.dot(next_ref[...], sigma, precision=HIGHEST, preferred_element_type=F32)
    for value, ref in ((mixed, sigma_ref), (green, earlier_ref)):
        for a in range(count):
            for c in range(2):
                part = value[c * times : (c + 1) * times, a * LANES : (a + 1) * LANES]
                turn[c, pl.ds(a, times, stride=count), :] = part
        for c in range(2):
            ref[0, c] = turn[c].astype(BF16)


def middle(first_orbital, scalars, coupling, keep, one, two, three, solve, following):
    rows = three.shape[1]
    strip = pl.BlockSpec((2, rows, LANES), lambda i: (0, 0, 0))
    square = pl.BlockSpec(solve.shape, lambda i: (0, 0))
    share = pl.BlockSpec((1, 2, rows, LANES), lambda i: (0, 0, 0, 0))
    scalar = pl.BlockSpec(memory_space=pltpu.SMEM)
    return pl.pallas_call(
        functools.partial(middle_body, first_orbital),
        out_shape=[jax.ShapeDtypeStruct((1, 2, rows, LANES), BF16)] * 2,
        grid=(1,),
        in_specs=[scalar, scalar] + [strip] * 4 + [square] * 2,
        out_specs=[share, share],
        scratch_shapes=[pltpu.VMEM((2, rows, LANES), F32)],
        compiler_params=pltpu.CompilerParams(vmem_limit_bytes=24 << 20),
        cost_estimate=pl.CostEstimate(flops=1 << 30, bytes_accessed=4 << 20, transcendentals=0),
        name="middle",
    )(scalars, coupling, keep, one, two, three, solve, following)


def second_body(start, count, low_ref, high_ref, near_ref, far_ref, out_ref, left):
    blocks = low_ref.shape[0]
    span = blocks * LANES
    depth = 2 * span

    @pl.when(pl.program_id(0) == 0)
    def _():
        for at, ref in ((0, low_ref), (span, high_ref)):
            for b in range(blocks):
                real = ref[b, 0, start : start + count, :]
                imag = ref[b, 1, start : start + count, :]
                here = pl.ds(at + b * LANES, LANES)
                there = pl.ds(depth + at + b * LANES, LANES)
                left[:count, here] = -real
                left[:count, there] = -imag
                left[count:, here] = -imag
                left[count:, there] = real

    def term(at, tile):
        return lax.dot_general(
            left[:, at : at + span], tile, (((1,), (1,)), ((), ())), preferred_element_type=F32
        )

    out = term(0, near_ref[0]) + term(span, far_ref[0])
    out += term(depth, near_ref[1]) + term(depth + span, far_ref[1])
    out_ref[0] = out[:count].astype(out_ref.dtype)
    out_ref[1] = out[count:].astype(out_ref.dtype)


def second_product(low, high, near, far, start, count, kind):
    depth, width = near.shape[1:]
    tile = 256
    whole = pl.BlockSpec(low.shape, lambda s: (0, 0, 0, 0))
    strip = pl.BlockSpec((2, tile, width), lambda s: (0, s, 0))
    return pl.pallas_call(
        functools.partial(second_body, start, count),
        out_shape=jax.ShapeDtypeStruct((2, count, depth), kind),
        grid=(depth // tile,),
        in_specs=[whole, whole, strip, strip],
        out_specs=pl.BlockSpec((2, count, tile), lambda s: (0, 0, s)),
        scratch_shapes=[pltpu.VMEM((2 * count, 4 * width), BF16)],
        compiler_params=pltpu.CompilerParams(vmem_limit_bytes=40 << 20),
        cost_estimate=pl.CostEstimate(
            flops=16 * count * width * depth, bytes_accessed=8 << 20, transcendentals=0
        ),
        name="second_product",
    )(low, high, near, far)


def assemble_body(scalars, *refs):
    out_ref = refs[-1]
    half = len(refs) // 2
    times, orbitals = out_ref.shape[1:3]
    width = orbitals // 2
    core = scalars[3]
    for at, group in ((core, refs[:half]), (1 - core, refs[half:-1])):
        per_chunk = width // half
        for k, ref in enumerate(group):
            for c in range(2):
                value = ref[0, c].astype(F32).reshape(times, per_chunk, LANES)
                row = pl.multiple_of(at * width + k * per_chunk, 8)
                out_ref[c, :, pl.ds(row, per_chunk), :] = value


def assemble_earlier(scalars, mine, others, times, orbitals):
    rows = mine[0].shape[2]
    blocks = mine[0].shape[0]
    own = pl.BlockSpec((1, 2, rows, LANES), lambda j, s: (s[0] ^ j, 0, 0, 0))
    other = pl.BlockSpec((1, 2, rows, LANES), lambda j, s: (s[1] ^ j, 0, 0, 0))
    return pl.pallas_call(
        assemble_body,
        out_shape=jax.ShapeDtypeStruct((2, times, orbitals, blocks * LANES), F32),
        grid_spec=pltpu.PrefetchScalarGridSpec(
            num_scalar_prefetch=1,
            grid=(blocks,),
            in_specs=[own] * len(mine) + [other] * len(others),
            out_specs=pl.BlockSpec((2, times, orbitals, LANES), lambda j, s: (0, 0, 0, j)),
        ),
        compiler_params=pltpu.CompilerParams(vmem_limit_bytes=40 << 20),
        cost_estimate=pl.CostEstimate(flops=0, bytes_accessed=12 << 20, transcendentals=0),
        name="assemble_earlier",
    )(scalars, *mine, *others)


def one_hot(position, count):
    return (position[:, None] == jnp.arange(count, dtype=jnp.int32)[None, :]).astype(F32)


def exact_dot(left, right):
    return jnp.dot(left, right, precision=HIGHEST, preferred_element_type=F32)


def later_body(scalars, *refs):
    out_ref = refs[-1]
    orbitals = out_ref.shape[2]
    count = refs[0].shape[2]
    half = orbitals // 2
    core = scalars[3]
    chunks = (len(refs) - 1) // 6
    for k in range(chunks):
        keep, one, two, three, across, far_across = refs[6 * k : 6 * k + 6]
        own_row = pl.multiple_of(core * half + k * count, 8)
        other_row = pl.multiple_of((1 - core) * half + k * count, 8)
        for c in range(2):
            for n in range(out_ref.shape[1]):
                total = keep[c, n] + one[c, n].astype(F32) + two[c, n].astype(F32) + three[c, n].astype(F32)
                out_ref[c, n, pl.ds(own_row, count), :] = TIME_STEP * total
                total = across[c, n].astype(F32) + far_across[c, n].astype(F32)
                out_ref[c, n, pl.ds(other_row, count), :] = TIME_STEP * total


def assemble_later(scalars, parts, own_times, orbitals):
    count, width = parts[0].shape[2:]
    tile = 256
    spec = pl.BlockSpec((2, own_times, count, tile), lambda t: (0, 0, 0, t))
    return pl.pallas_call(
        later_body,
        out_shape=jax.ShapeDtypeStruct((2, own_times, orbitals, width), F32),
        grid=(width // tile,),
        in_specs=[pl.BlockSpec(memory_space=pltpu.SMEM)] + [spec] * len(parts),
        out_specs=pl.BlockSpec((2, own_times, orbitals, tile), lambda t: (0, 0, 0, t)),
        compiler_params=pltpu.CompilerParams(vmem_limit_bytes=24 << 20),
        cost_estimate=pl.CostEstimate(flops=1 << 20, bytes_accessed=5 << 20, transcendentals=0),
        name="assemble_later",
    )(scalars, *parts)


def paired(real, imag):
    return jnp.concatenate(
        [jnp.concatenate([real, -imag], axis=1), jnp.concatenate([imag, real], axis=1)], axis=0
    )


def shards(history, start_strip, coupling, dyson_inverse):
    orbitals = coupling.shape[0]
    times = dyson_inverse.shape[2]
    yl, x, z, yh, core = [lax.axis_index(a) for a in AXES]
    strip_rows, strip_cols = start_strip.shape[1:]
    own_times = strip_rows // orbitals
    half = orbitals // 2
    per_chunk = half // CHUNKS
    chip_times = 2 * own_times
    block_rows = chip_times * per_chunk
    rows = times * per_chunk
    tile_cols = history.shape[2]

    row_place = place_of(yl, x, core)
    other_row_place = place_of(yl, x, 1 - core)
    col_place = place_of(yh, z, core)
    own_near = (row_place >> 2) == core
    scalars = jnp.stack(
        [row_place & 3, other_row_place & 3, own_near.astype(jnp.int32), core]
    ).astype(jnp.int32)

    strip = start_strip.reshape(2, own_times, orbitals, strip_cols)
    sigma_own, sigma_other = sigma_strip(scalars, coupling, strip)
    sigma_core = send(sigma_other, CORE_STEP)
    sigma_next = send(sigma_own, COL_STEPS[0])
    sigma_across = send(sigma_other, COL_ACROSS_IN)
    other_history = send(history, CORE_STEP)
    near, far = arrange_history(scalars, history, other_history)

    block = jnp.arange(8, dtype=jnp.int32)
    group = ring_group(col_place ^ block, core)
    inner = (jnp.arange(chip_times, dtype=jnp.int32) + own_times * core) % chip_times
    time_order = (chip_times * group[:, None] + inner[None, :]).reshape(-1)
    order = one_hot(time_order, times)
    solve = paired(exact_dot(dyson_inverse[0, 0], order.T), exact_dot(dyson_inverse[0, 1], order.T))
    following = paired(exact_dot(order, dyson_inverse[1, 0]), exact_dot(order, dyson_inverse[1, 1]))

    later_parts = []
    mine = []
    others = []
    for k in range(CHUNKS):
        chunk = slice(k * per_chunk, (k + 1) * per_chunk)
        joined = jnp.stack(
            [
                jnp.concatenate([p[:, :, chunk] for p in pair], axis=1)
                for pair in ((sigma_own, sigma_core), (sigma_next, sigma_across))
            ]
        ).reshape(2, 2, block_rows, strip_cols)
        low = jnp.concatenate([joined, send(joined, COL_STEPS[1])], axis=0)
        high = send(low, COL_STEPS[2])
        away = first_product(low, high, far, BF16)
        one = send(away, ROW_STEPS[2])
        keep = first_product(low, high, near, F32)
        width = tile_cols // 2
        two_out = (keep[:, :, width:] + one[:, :, width:].astype(F32)).astype(BF16)
        two = send(two_out, ROW_STEPS[1])
        span = slice(LANES, 2 * LANES)
        three_out = keep[:, :, span] + one[:, :, span].astype(F32) + two[:, :, span].astype(F32)
        three = send(three_out.astype(BF16), ROW_STEPS[0])
        earlier_share, sigma_share = middle(
            k * per_chunk, scalars, coupling, keep, one, two, three, solve, following
        )

        low, high = gather_steps(sigma_share, ROW_STEPS)
        away = second_product(low, high, near, far, rows // 2, rows // 2, BF16)
        one = send(away, COL_STEPS[2])
        keep = second_product(low, high, near, far, 0, rows // 2, F32)
        size = rows // 4
        two_out = (keep[:, size:] + one[:, size:].astype(F32)).astype(BF16)
        two = send(two_out, COL_STEPS[1])
        sums = [
            v[:, : 2 * block_rows].reshape(2, 4, own_times, per_chunk, strip_cols) for v in (keep, one, two)
        ]
        outgoing = [
            (sums[0][:, i] + sums[1][:, i].astype(F32) + sums[2][:, i].astype(F32)).astype(kind)
            for i, kind in ((1, F32), (2, BF16), (3, BF16))
        ]
        core_sum = send(outgoing[0], CORE_STEP)
        three = send(outgoing[1], COL_STEPS[0])
        across = send(outgoing[2], COL_ACROSS_OUT)
        later_parts += [v[:, 0] for v in sums] + [three, core_sum, across]

        earlier_share, _ = lax.optimization_barrier((earlier_share, high))
        low, high = gather_steps(earlier_share, ROW_STEPS)
        mine.append(jnp.where(own_near, low, high))
        others.append(send(jnp.where(own_near, high, low), CORE_STEP))

    earlier = assemble_earlier(scalars, mine, others, times, orbitals)
    later = assemble_later(scalars, later_parts, own_times, orbitals)
    return (
        earlier.reshape(2, times * orbitals, tile_cols),
        later.reshape(2, strip_rows, strip_cols),
    )


def solution(mesh):
    finer = Mesh(mesh.devices.reshape(SIZES), AXES)
    in_specs = (P(None, ROW, COL), P(None, COL, ROW), P(), P())
    out_specs = (P(None, None, COL), P(None, COL, ROW))
    return jax.shard_map(
        shards, mesh=finer, in_specs=in_specs, out_specs=out_specs, check_vma=False
    )
```

```python
import functools

import jax
import jax.numpy as jnp
from jax import lax
from jax.experimental import pallas as pl
from jax.experimental.pallas import tpu as pltpu
from jax.sharding import Mesh
from jax.sharding import PartitionSpec as P

AXES = ("yl", "x", "z", "yh", "core")
SIZES = (2, 4, 4, 2, 2)
ROW = ("yl", "x")
COL = ("z", "yh", "core")
TIME_STEP = 0.15
BITS = ((0, 1, 2), (0, 1, 2))
CHUNKS = len(BITS)
LANES = 128
BF16 = jnp.bfloat16
F32 = jnp.float32
HIGHEST = lax.Precision.HIGHEST


def coordinates(flat):
    found = []
    for size in reversed(SIZES):
        found.append(flat % size)
        flat //= size
    return dict(zip(AXES, reversed(found)))


def flat_index(where):
    flat = 0
    for name, size in zip(AXES, SIZES):
        flat = flat * size + where[name]
    return flat


def pairs(change):
    devices = 1
    for size in SIZES:
        devices *= size
    out = []
    for device in range(devices):
        where = coordinates(device)
        out.append((device, flat_index({**where, **change(where)})))
    return out


def ring_pairs(ring, second):
    return pairs(lambda w: {ring: w[ring] ^ (3 if (w["core"] == 1) != second else 1)})


ROW_STEPS = (
    pairs(lambda w: {"yl": w["yl"] ^ 1}),
    ring_pairs("x", False),
    ring_pairs("x", True),
)
COL_STEPS = (
    pairs(lambda w: {"yh": w["yh"] ^ 1}),
    ring_pairs("z", False),
    ring_pairs("z", True),
)
CORE_STEP = pairs(lambda w: {"core": w["core"] ^ 1})
COL_ACROSS = pairs(lambda w: {"core": w["core"] ^ 1, "yh": w["yh"] ^ 1})


def send(value, step):
    return lax.ppermute(value, AXES, step)


def place_of(low, ring, core):
    first = (ring ^ (ring >> 1)) & 1
    second = ring >> 1
    swap = core == 1
    return low + 2 * jnp.where(swap, second, first) + 4 * jnp.where(swap, first, second)


def ring_group(place, core):
    low = place & 1
    one = (place >> 1) & 1
    two = (place >> 2) & 1
    swap = core == 1
    first = jnp.where(swap, two, one)
    second = jnp.where(swap, one, two)
    return 2 * (2 * second + (first ^ second)) + low


class Line:
    def __init__(self):
        self.last = []

    def call(self, body, out_shape, operands, specs, out_specs, name, megabytes, flops, grid=(), scratch=(), scalars=None):
        count = len(operands) + (scalars is not None)
        extra = len(self.last)

        def wrapped(*refs):
            body(*refs[:count], *refs[count + extra :])

        any_spec = [pl.BlockSpec(memory_space=pl.ANY)] * extra
        common = dict(
            out_shape=out_shape,
            compiler_params=pltpu.CompilerParams(vmem_limit_bytes=40 << 20),
            cost_estimate=pl.CostEstimate(
                flops=0, bytes_accessed=1024, transcendentals=0
            ),
            name=name,
        )
        if scalars is None:
            called = pl.pallas_call(
                wrapped, grid=grid, in_specs=specs + any_spec, out_specs=out_specs,
                scratch_shapes=list(scratch), **common,
            )
            outs = called(*operands, *self.last)
        else:
            grid_spec = pltpu.PrefetchScalarGridSpec(
                num_scalar_prefetch=1, grid=grid, in_specs=specs + any_spec, out_specs=out_specs
            )
            called = pl.pallas_call(wrapped, grid_spec=grid_spec, **common)
            outs = called(scalars, *operands, *self.last)
        self.last = [outs[0] if isinstance(outs, (list, tuple)) else outs]
        return outs


WHOLE = pl.BlockSpec(memory_space=pltpu.VMEM)
SCALAR = pl.BlockSpec(memory_space=pltpu.SMEM)


def join_body(axis, count, *refs):
    out_ref = refs[-1]
    at = 0
    for ref in refs[:count]:
        size = ref.shape[axis]
        out_ref[(slice(None),) * axis + (slice(at, at + size),)] = ref[...]
        at += size


def join(line, parts, axis=0):
    shape = list(parts[0].shape)
    shape[axis] = sum(p.shape[axis] for p in parts)
    return line.call(
        functools.partial(join_body, axis, len(parts)),
        jax.ShapeDtypeStruct(tuple(shape), parts[0].dtype),
        parts, [WHOLE] * len(parts), WHOLE, "join", 2, 0,
    )


def fold_body(index, *refs):
    total = refs[0][index].astype(F32)
    for ref in refs[1:-1]:
        total += ref[index].astype(F32)
    refs[-1][...] = total.astype(refs[-1].dtype)


def fold(line, parts, axis, start, stop):
    shape = list(parts[0].shape)
    shape[axis] = stop - start
    index = (slice(None),) * axis + (slice(start, stop),)
    return line.call(
        functools.partial(fold_body, index),
        jax.ShapeDtypeStruct(tuple(shape), BF16),
        parts, [WHOLE] * len(parts), WHOLE, "fold", 3, 1 << 20,
    )


def finish_body(*refs):
    own_ref, sent_ref = refs[-2:]
    rows = own_ref.shape[2]
    for k in range(CHUNKS):
        keep, one, two, three = refs[4 * k : 4 * k + 4]
        for at, ref in ((0, own_ref), (rows, sent_ref)):
            here = (slice(None), slice(at, at + rows))
            total = keep[here] + one[here].astype(F32) + two[here].astype(F32) + three[here].astype(F32)
            ref[k] = TIME_STEP * total


def finish(line, parts):
    rows, width = parts[3].shape[1:]
    out = jax.ShapeDtypeStruct((CHUNKS, 2, rows // 2, width), F32)
    return line.call(
        finish_body, [out, out], parts, [WHOLE] * len(parts), [WHOLE] * 2, "finish", 4, 1 << 20
    )


def blocks_body(k, count, *refs):
    out_ref = refs[-1]
    own_times = refs[0].shape[1]
    for i in range(4):
        for c in range(2):
            for n in range(own_times):
                row = ((i % 2) * own_times + n) * count
                value = refs[i][c, n].astype(F32)[k * count : (k + 1) * count]
                out_ref[i // 2, c, row : row + count] = value.astype(BF16)


def as_blocks(line, parts, k, count):
    own_times, _, width = parts[0].shape[1:]
    return line.call(
        functools.partial(blocks_body, k, count),
        jax.ShapeDtypeStruct((2, 2, 2 * own_times * count, width), BF16),
        parts, [WHOLE] * 4, WHOLE, "blocks", 2, 0,
    )


def arrange_body(scalars, own_ref, other_ref, near_ref, far_ref):
    own_near = scalars[2] == 1

    @pl.when(own_near)
    def _():
        near_ref[...] = own_ref[...]
        far_ref[...] = other_ref[...]

    @pl.when(jnp.logical_not(own_near))
    def _():
        near_ref[...] = other_ref[...]
        far_ref[...] = own_ref[...]


def arrange_history(line, scalars, own, other):
    depth, width = own.shape[1:]
    spec_in = pl.BlockSpec((2, depth, LANES), lambda j, s: (0, 0, s[0] ^ j))
    spec_out = pl.BlockSpec((2, depth, LANES), lambda j, s: (0, 0, j))
    return line.call(
        arrange_body,
        [jax.ShapeDtypeStruct(own.shape, BF16)] * 2,
        [own, other], [spec_in, spec_in], [spec_out, spec_out], "arrange_history", 8, 0,
        grid=(width // LANES,), scalars=scalars,
    )


def tile_of(near_ref, far_ref, c, block):
    blocks = near_ref.shape[2] // LANES
    ref = near_ref if block < blocks else far_ref
    at = (block % blocks) * LANES
    return ref[c, :, at : at + LANES]


def first_body(order, low_ref, high_ref, near_ref, far_ref, out_ref):
    blocks, _, rows, depth = low_ref.shape
    span = 2 * LANES
    for p in range(len(order) // 2):
        tiles = [
            jnp.concatenate([tile_of(near_ref, far_ref, c, b) for b in order[2 * p : 2 * p + 2]], axis=1)
            for c in range(2)
        ]
        for at, ref in ((0, low_ref), (blocks * rows, high_ref)):
            left = ref[...].reshape(2 * blocks * rows, depth)
            by_real = jnp.dot(left, tiles[0], preferred_element_type=F32)
            by_imag = jnp.dot(left, tiles[1], preferred_element_type=F32)
            for b in range(blocks):
                real = slice(2 * b * rows, (2 * b + 1) * rows)
                imag = slice((2 * b + 1) * rows, (2 * b + 2) * rows)
                put = (slice(at + b * rows, at + (b + 1) * rows), slice(p * span, (p + 1) * span))
                out_ref[0, put[0], put[1]] = (by_real[real] - by_imag[imag]).astype(out_ref.dtype)
                out_ref[1, put[0], put[1]] = (by_real[imag] + by_imag[real]).astype(out_ref.dtype)


def first_product(line, low, high, near, far, order, kind):
    blocks, _, rows, depth = low.shape
    full = 2 * blocks * rows
    width = len(order) * LANES
    return line.call(
        functools.partial(first_body, order),
        jax.ShapeDtypeStruct((2, full, width), kind),
        [low, high, near, far], [WHOLE] * 4, WHOLE, "first_product", 8, 8 * full * depth * width,
    )


def lane_weights(coupling, shape, axis):
    orbitals = coupling.shape[0]
    at = lax.rem(lax.broadcasted_iota(jnp.int32, shape, axis), orbitals)
    weights = jnp.zeros(shape, F32)
    for a in range(orbitals):
        weights = jnp.where(at == a, coupling[a], weights)
    return weights


def sigma_body(scalars, coupling, strip_ref, own_ref, other_ref):
    _, own_times, orbitals, width = strip_ref.shape
    half = orbitals // 2
    core = scalars[3]
    col = lane_weights(coupling, (1, LANES), 1)
    col = jnp.concatenate([col] * (width // LANES), axis=1)
    row = lane_weights(coupling, (orbitals, LANES), 0)
    row = jnp.concatenate([row] * (width // LANES), axis=1)
    weight = row * col
    for n in range(own_times):
        real = strip_ref[0, n]
        imag = strip_ref[1, n]
        factor = -weight * (real * real + imag * imag)
        for c, part in ((0, real), (1, imag)):
            sigma = part * factor
            first, second = sigma[:half], sigma[half:]
            own = jnp.where(core == 0, first, second)
            other = jnp.where(core == 0, second, first)
            own_ref[c, n] = own.astype(BF16)
            other_ref[c, n] = other.astype(BF16)


def sigma_strip(scalars, coupling, strip):
    _, own_times, orbitals, width = strip.shape
    out = jax.ShapeDtypeStruct((2, own_times, orbitals // 2, width), BF16)
    return pl.pallas_call(
        sigma_body,
        out_shape=[out, out],
        in_specs=[
            pl.BlockSpec(memory_space=pltpu.SMEM),
            pl.BlockSpec(memory_space=pltpu.SMEM),
            pl.BlockSpec(memory_space=pltpu.VMEM),
        ],
        out_specs=[pl.BlockSpec(memory_space=pltpu.VMEM)] * 2,
        compiler_params=pltpu.CompilerParams(vmem_limit_bytes=24 << 20),
        cost_estimate=pl.CostEstimate(flops=3 << 20, bytes_accessed=3 << 20, transcendentals=0),
        name="sigma_strip",
    )(scalars, coupling, strip)


def middle_body(
    first_orbital, scalars, coupling, keep_ref, one_ref, two_ref, three_ref, solve_ref, next_ref, earlier_ref, sigma_ref, turn
):
    rows = three_ref.shape[1]
    times = solve_ref.shape[0] // 2
    count = rows // times
    orbitals = coupling.shape[0]
    for c in range(2):
        total = keep_ref[c, :, :LANES] + one_ref[c, :, :LANES].astype(F32)
        total += two_ref[c, :, :LANES].astype(F32) + three_ref[c].astype(F32)
        turn[c] = TIME_STEP * total

    def column(a):
        return jnp.concatenate([turn[c, pl.ds(a, times, stride=count), :] for c in range(2)], axis=0)

    source = jnp.concatenate([column(a) for a in range(count)], axis=1)
    green = jnp.dot(solve_ref[...], source, precision=HIGHEST, preferred_element_type=F32)
    col = lane_weights(coupling, (1, LANES), 1)
    base = scalars[3] * (orbitals // 2) + first_orbital
    weight = jnp.concatenate([-(coupling[base + a] * col) for a in range(count)], axis=1)
    real = green[:times]
    imag = green[times:]
    factor = weight * (real * real + imag * imag)
    sigma = jnp.concatenate([real * factor, imag * factor], axis=0)
    mixed = jnp.dot(next_ref[...], sigma, precision=HIGHEST, preferred_element_type=F32)
    for value, ref in ((mixed, sigma_ref), (green, earlier_ref)):
        for a in range(count):
            for c in range(2):
                part = value[c * times : (c + 1) * times, a * LANES : (a + 1) * LANES]
                turn[c, pl.ds(a, times, stride=count), :] = part
        for c in range(2):
            ref[0, c] = turn[c].astype(BF16)


def middle(line, first_orbital, scalars, coupling, keep, one, two, three, solve, following):
    rows = three.shape[1]
    share = jax.ShapeDtypeStruct((1, 2, rows, LANES), BF16)
    return line.call(
        functools.partial(middle_body, first_orbital),
        [share, share],
        [scalars, coupling, keep, one, two, three, solve, following],
        [SCALAR, SCALAR] + [WHOLE] * 6, [WHOLE, WHOLE], "middle", 4, 1 << 30,
        scratch=[pltpu.VMEM((2, rows, LANES), F32)],
    )


def second_body(start, order, low_ref, high_ref, near_ref, far_ref, out_ref, left):
    blocks = low_ref.shape[0]
    count = out_ref.shape[1]
    span = blocks * LANES
    tile = 256
    for i, b in enumerate(order):
        ref = low_ref if i < blocks else high_ref
        for c in range(2):
            left[c * count : (c + 1) * count, b * LANES : (b + 1) * LANES] = ref[
                i % blocks, c, start : start + count, :
            ]
    for s in range(out_ref.shape[2] // tile):
        here = slice(s * tile, (s + 1) * tile)

        def by(c):
            return sum(
                lax.dot_general(
                    left[:, at : at + span],
                    ref[c, here],
                    (((1,), (1,)), ((), ())),
                    preferred_element_type=F32,
                )
                for at, ref in ((0, near_ref), (span, far_ref))
            )

        by_real = by(0)
        by_imag = by(1)
        out_ref[0, :, here] = (-(by_real[:count] + by_imag[count:])).astype(out_ref.dtype)
        out_ref[1, :, here] = (by_imag[:count] - by_real[count:]).astype(out_ref.dtype)


def second_product(line, low, high, near, far, order, start, count, kind):
    depth, width = near.shape[1:]
    return line.call(
        functools.partial(second_body, start, order),
        jax.ShapeDtypeStruct((2, count, depth), kind),
        [low, high, near, far], [WHOLE] * 4, WHOLE, "second_product", 8, 16 * count * width * depth,
        scratch=[pltpu.VMEM((2 * count, 2 * width), BF16)],
    )


def split_tiles(line, scalars, near, far):
    out = jax.ShapeDtypeStruct(near.shape, near.dtype)
    return line.call(
        arrange_body, [out, out], [scalars, near, far], [SCALAR, WHOLE, WHOLE], [WHOLE] * 2, "split_tiles", 8, 0
    )


def assemble_body(scalars, mine_ref, others_ref, out_ref):
    times, orbitals = out_ref.shape[1:3]
    width = orbitals // 2
    core = scalars[3]
    per_chunk = width // CHUNKS
    for at, ref in ((core, mine_ref), (1 - core, others_ref)):
        for k in range(CHUNKS):
            for c in range(2):
                value = ref[0, k, c].astype(F32).reshape(times, per_chunk, LANES)
                row = pl.multiple_of(at * width + k * per_chunk, 8)
                out_ref[c, :, pl.ds(row, per_chunk), :] = value


def assemble_earlier(line, scalars, mine, others, times, orbitals):
    blocks = mine.shape[0]
    block = (1,) + mine.shape[1:]
    own = pl.BlockSpec(block, lambda j, s: (s[0] ^ j, 0, 0, 0, 0))
    other = pl.BlockSpec(block, lambda j, s: (s[1] ^ j, 0, 0, 0, 0))
    return line.call(
        assemble_body,
        jax.ShapeDtypeStruct((2, times, orbitals, blocks * LANES), F32),
        [mine, others], [own, other],
        pl.BlockSpec((2, times, orbitals, LANES), lambda j, s: (0, 0, 0, j)),
        "assemble_earlier", 12, 0, grid=(blocks,), scalars=scalars,
    )


def one_hot(position, count):
    return (position[:, None] == jnp.arange(count, dtype=jnp.int32)[None, :]).astype(F32)


def exact_dot(left, right):
    return jnp.dot(left, right, precision=HIGHEST, preferred_element_type=F32)


def later_body(scalars, own_ref, arrived_ref, out_ref):
    half = out_ref.shape[2] // 2
    count = own_ref.shape[3]
    core = scalars[3]
    for at, ref in ((core, own_ref), (1 - core, arrived_ref)):
        for k in range(CHUNKS):
            row = pl.multiple_of(at * half + k * count, 8)
            for c in range(2):
                for n in range(out_ref.shape[1]):
                    out_ref[c, n, pl.ds(row, count), :] = ref[k, c, n]


def assemble_later(line, scalars, own, arrived, orbitals):
    _, _, own_times, count, width = own.shape
    tile = 256
    spec = pl.BlockSpec((CHUNKS, 2, own_times, count, tile), lambda t: (0, 0, 0, 0, t))
    return line.call(
        later_body,
        jax.ShapeDtypeStruct((2, own_times, orbitals, width), F32),
        [scalars, own, arrived], [SCALAR, spec, spec],
        pl.BlockSpec((2, own_times, orbitals, tile), lambda t: (0, 0, 0, t)),
        "assemble_later", 5, 1 << 20, grid=(width // tile,),
    )


def paired(real, imag):
    return jnp.concatenate(
        [jnp.concatenate([real, -imag], axis=1), jnp.concatenate([imag, real], axis=1)], axis=0
    )


def block_order(bits):
    order = [0]
    for bit in bits:
        order += [b + (1 << bit) for b in order]
    return tuple(order)


def shards(history, start_strip, coupling, dyson_inverse):
    orbitals = coupling.shape[0]
    times = dyson_inverse.shape[2]
    yl, x, z, yh, core = [lax.axis_index(a) for a in AXES]
    strip_rows, strip_cols = start_strip.shape[1:]
    own_times = strip_rows // orbitals
    per_chunk = orbitals // 2 // CHUNKS
    chip_times = 2 * own_times
    block_rows = chip_times * per_chunk
    rows = times * per_chunk
    tile_cols = history.shape[2]

    row_place = place_of(yl, x, core)
    other_row_place = place_of(yl, x, 1 - core)
    col_place = place_of(yh, z, core)
    own_near = (row_place >> 2) == core
    scalars = jnp.stack(
        [row_place & 3, other_row_place & 3, own_near.astype(jnp.int32), core]
    ).astype(jnp.int32)

    strip = start_strip.reshape(2, own_times, orbitals, strip_cols)
    sigma_own, sigma_other = sigma_strip(scalars, coupling, strip)
    sigma_core = send(sigma_other, CORE_STEP)
    sigma_next = send(sigma_own, COL_STEPS[0])
    sigma_across = send(sigma_other, COL_ACROSS)
    other_history = send(history, CORE_STEP)
    inner = (jnp.arange(chip_times, dtype=jnp.int32) + own_times * core) % chip_times
    matrices = {}
    for bits in sorted(set(BITS)):
        group = ring_group(col_place ^ jnp.array(block_order(bits), jnp.int32), core)
        order = one_hot((chip_times * group[:, None] + inner[None, :]).reshape(-1), times)
        solve = paired(exact_dot(dyson_inverse[0, 0], order.T), exact_dot(dyson_inverse[0, 1], order.T))
        following = paired(exact_dot(order, dyson_inverse[1, 0]), exact_dot(order, dyson_inverse[1, 1]))
        matrices[bits] = (solve, following)

    line = Line()
    chunks = range(CHUNKS)
    orders = [block_order(bits) for bits in BITS]
    quarter = tile_cols // 4
    parts = (sigma_own, sigma_core, sigma_next, sigma_across)
    low, arriving, high, away, keep, one, two, three = ([None] * CHUNKS for _ in range(8))
    for k in chunks:
        low[k] = as_blocks(line, parts, k, per_chunk)
        arriving[k] = send(low[k], COL_STEPS[BITS[k][1]])
    near, far = arrange_history(line, scalars, history, other_history)
    for k in chunks:
        low[k] = join(line, [low[k], arriving[k]])
        high[k] = send(low[k], COL_STEPS[BITS[k][2]])
    for k in chunks:
        away[k] = first_product(line, low[k], high[k], near, far, orders[k][4:], BF16)
        one[k] = send(away[k], ROW_STEPS[BITS[k][2]])
        keep[k] = first_product(line, low[k], high[k], near, far, orders[k][:4], F32)
    for k in chunks:
        out = fold(line, [keep[k], one[k]], 2, 2 * quarter, 4 * quarter)
        two[k] = send(out, ROW_STEPS[BITS[k][1]])
    for k in chunks:
        out = fold(line, [keep[k], one[k], two[k]], 2, quarter, 2 * quarter)
        three[k] = send(out, ROW_STEPS[BITS[k][0]])
    share, earlier_share = [None] * CHUNKS, [None] * CHUNKS
    for k in chunks:
        earlier_share[k], share[k] = middle(
            line, k * per_chunk, scalars, coupling, keep[k], one[k], two[k], three[k], *matrices[BITS[k]]
        )
        arriving[k] = send(share[k], ROW_STEPS[BITS[k][0]])

    for k in chunks:
        low[k] = join(line, [share[k], arriving[k]])
        arriving[k] = send(low[k], ROW_STEPS[BITS[k][1]])
    for k in chunks:
        low[k] = join(line, [low[k], arriving[k]])
        high[k] = send(low[k], ROW_STEPS[BITS[k][2]])
    for k in chunks:
        away[k] = second_product(line, low[k], high[k], near, far, orders[k], rows // 2, rows // 2, BF16)
        one[k] = send(away[k], COL_STEPS[BITS[k][2]])
        keep[k] = second_product(line, low[k], high[k], near, far, orders[k], 0, rows // 2, F32)
    earlier = join(line, [e[:, None] for e in earlier_share], axis=1)
    earlier_next = send(earlier, ROW_STEPS[0])
    out = fold(line, [keep[0], one[0]], 1, 2 * block_rows, 4 * block_rows)
    two[0] = send(out, COL_STEPS[BITS[0][1]])
    earlier = join(line, [earlier, earlier_next])
    earlier_next = send(earlier, ROW_STEPS[1])
    out = fold(line, [keep[1], one[1]], 1, 2 * block_rows, 4 * block_rows)
    two[1] = send(out, COL_STEPS[BITS[1][1]])
    out = fold(line, [keep[0], one[0], two[0]], 1, block_rows, 2 * block_rows)
    three[0] = send(out, COL_STEPS[BITS[0][0]])
    earlier = join(line, [earlier, earlier_next])
    earlier_next = send(earlier, ROW_STEPS[2])
    out = fold(line, [keep[1], one[1], two[1]], 1, block_rows, 2 * block_rows)
    three[1] = send(out, COL_STEPS[BITS[1][0]])
    own, sent = finish(line, [v for k in chunks for v in (keep[k], one[k], two[k], three[k])])
    arrived = send(sent, CORE_STEP)
    split = (CHUNKS, 2, own_times, per_chunk, strip_cols)
    later = assemble_later(line, scalars, own.reshape(split), arrived.reshape(split), orbitals)
    mine, others = split_tiles(line, scalars, earlier, earlier_next)
    others = send(others, CORE_STEP)
    earlier = assemble_earlier(line, scalars, mine, others, times, orbitals)
    return (
        earlier.reshape(2, times * orbitals, tile_cols),
        later.reshape(2, strip_rows, strip_cols),
    )


def solution(mesh):
    finer = Mesh(mesh.devices.reshape(SIZES), AXES)
    in_specs = (P(None, ROW, COL), P(None, COL, ROW), P(), P())
    out_specs = (P(None, None, COL), P(None, COL, ROW))
    return jax.shard_map(
        shards, mesh=finer, in_specs=in_specs, out_specs=out_specs, check_vma=False
    )
```

```python
import functools

import jax
import jax.numpy as jnp
from jax import lax
from jax.experimental import pallas as pl
from jax.experimental.pallas import tpu as pltpu
from jax.sharding import Mesh
from jax.sharding import PartitionSpec as P

AXES = ("yl", "x", "z", "yh", "core")
SIZES = (2, 4, 4, 2, 2)
ROW = ("yl", "x")
COL = ("z", "yh", "core")
TIME_STEP = 0.15
BITS = ((0, 1, 2), (0, 1, 2))
CHUNKS = len(BITS)
LANES = 128
BF16 = jnp.bfloat16
F32 = jnp.float32
HIGHEST = lax.Precision.HIGHEST


def coordinates(flat):
    found = []
    for size in reversed(SIZES):
        found.append(flat % size)
        flat //= size
    return dict(zip(AXES, reversed(found)))


def flat_index(where):
    flat = 0
    for name, size in zip(AXES, SIZES):
        flat = flat * size + where[name]
    return flat


def pairs(change):
    devices = 1
    for size in SIZES:
        devices *= size
    out = []
    for device in range(devices):
        where = coordinates(device)
        out.append((device, flat_index({**where, **change(where)})))
    return out


def ring_pairs(ring, second):
    return pairs(lambda w: {ring: w[ring] ^ (3 if (w["core"] == 1) != second else 1)})


ROW_STEPS = (
    pairs(lambda w: {"yl": w["yl"] ^ 1}),
    ring_pairs("x", False),
    ring_pairs("x", True),
)
COL_STEPS = (
    pairs(lambda w: {"yh": w["yh"] ^ 1}),
    ring_pairs("z", False),
    ring_pairs("z", True),
)
CORE_STEP = pairs(lambda w: {"core": w["core"] ^ 1})
COL_ACROSS = pairs(lambda w: {"core": w["core"] ^ 1, "yh": w["yh"] ^ 1})


def send(value, step):
    return lax.ppermute(value, AXES, step)


def place_of(low, ring, core):
    first = (ring ^ (ring >> 1)) & 1
    second = ring >> 1
    swap = core == 1
    return low + 2 * jnp.where(swap, second, first) + 4 * jnp.where(swap, first, second)


def ring_group(place, core):
    low = place & 1
    one = (place >> 1) & 1
    two = (place >> 2) & 1
    swap = core == 1
    first = jnp.where(swap, two, one)
    second = jnp.where(swap, one, two)
    return 2 * (2 * second + (first ^ second)) + low


class Line:
    def __init__(self):
        self.last = []

    def call(self, body, out_shape, operands, specs, out_specs, name, megabytes, flops, grid=(), scratch=(), scalars=None):
        count = len(operands) + (scalars is not None)
        extra = len(self.last)

        def wrapped(*refs):
            body(*refs[:count], *refs[count + extra :])

        any_spec = [pl.BlockSpec(memory_space=pl.ANY)] * extra
        common = dict(
            out_shape=out_shape,
            compiler_params=pltpu.CompilerParams(vmem_limit_bytes=40 << 20),
            cost_estimate=pl.CostEstimate(
                flops=0, bytes_accessed=1024, transcendentals=0
            ),
            name=name,
        )
        if scalars is None:
            called = pl.pallas_call(
                wrapped, grid=grid, in_specs=specs + any_spec, out_specs=out_specs,
                scratch_shapes=list(scratch), **common,
            )
            outs = called(*operands, *self.last)
        else:
            grid_spec = pltpu.PrefetchScalarGridSpec(
                num_scalar_prefetch=1, grid=grid, in_specs=specs + any_spec, out_specs=out_specs
            )
            called = pl.pallas_call(wrapped, grid_spec=grid_spec, **common)
            outs = called(scalars, *operands, *self.last)
        self.last = [outs[0] if isinstance(outs, (list, tuple)) else outs]
        return outs


WHOLE = pl.BlockSpec(memory_space=pltpu.VMEM)
SCALAR = pl.BlockSpec(memory_space=pltpu.SMEM)


def join_body(axis, count, *refs):
    out_ref = refs[-1]
    at = 0
    for ref in refs[:count]:
        size = ref.shape[axis]
        out_ref[(slice(None),) * axis + (slice(at, at + size),)] = ref[...]
        at += size


def join(line, parts, axis=0):
    shape = list(parts[0].shape)
    shape[axis] = sum(p.shape[axis] for p in parts)
    return line.call(
        functools.partial(join_body, axis, len(parts)),
        jax.ShapeDtypeStruct(tuple(shape), parts[0].dtype),
        parts, [WHOLE] * len(parts), WHOLE, "join", 2, 0,
    )


def fold_body(index, *refs):
    total = refs[0][index].astype(F32)
    for ref in refs[1:-1]:
        total += ref[index].astype(F32)
    refs[-1][...] = total.astype(refs[-1].dtype)


def fold(line, parts, axis, start, stop):
    shape = list(parts[0].shape)
    shape[axis] = stop - start
    index = (slice(None),) * axis + (slice(start, stop),)
    return line.call(
        functools.partial(fold_body, index),
        jax.ShapeDtypeStruct(tuple(shape), BF16),
        parts, [WHOLE] * len(parts), WHOLE, "fold", 3, 1 << 20,
    )


def finish_body(*refs):
    own_ref, sent_ref = refs[-2:]
    rows = own_ref.shape[2]
    for k in range(CHUNKS):
        keep, one, two, three = refs[4 * k : 4 * k + 4]
        for at, ref in ((0, own_ref), (rows, sent_ref)):
            here = (slice(None), slice(at, at + rows))
            total = keep[here] + one[here].astype(F32) + two[here].astype(F32) + three[here].astype(F32)
            ref[k] = TIME_STEP * total


def finish(line, parts):
    rows, width = parts[3].shape[1:]
    out = jax.ShapeDtypeStruct((CHUNKS, 2, rows // 2, width), F32)
    return line.call(
        finish_body, [out, out], parts, [WHOLE] * len(parts), [WHOLE] * 2, "finish", 4, 1 << 20
    )


def blocks_body(k, count, *refs):
    out_ref = refs[-1]
    own_times = refs[0].shape[1]
    for i in range(4):
        for c in range(2):
            for n in range(own_times):
                row = ((i % 2) * own_times + n) * count
                value = refs[i][c, n].astype(F32)[k * count : (k + 1) * count]
                out_ref[i // 2, c, row : row + count] = value.astype(BF16)


def as_blocks(line, parts, k, count):
    own_times, _, width = parts[0].shape[1:]
    return line.call(
        functools.partial(blocks_body, k, count),
        jax.ShapeDtypeStruct((2, 2, 2 * own_times * count, width), BF16),
        parts, [WHOLE] * 4, WHOLE, "blocks", 2, 0,
    )


def arrange_body(scalars, own_ref, other_ref, near_ref, far_ref):
    own_near = scalars[2] == 1

    @pl.when(own_near)
    def _():
        near_ref[...] = own_ref[...]
        far_ref[...] = other_ref[...]

    @pl.when(jnp.logical_not(own_near))
    def _():
        near_ref[...] = other_ref[...]
        far_ref[...] = own_ref[...]


def arrange_history(line, scalars, own, other):
    depth, width = own.shape[1:]
    spec_in = pl.BlockSpec((2, depth, LANES), lambda j, s: (0, 0, s[0] ^ j))
    spec_out = pl.BlockSpec((2, depth, LANES), lambda j, s: (0, 0, j))
    return line.call(
        arrange_body,
        [jax.ShapeDtypeStruct(own.shape, BF16)] * 2,
        [own, other], [spec_in, spec_in], [spec_out, spec_out], "arrange_history", 8, 0,
        grid=(width // LANES,), scalars=scalars,
    )


def tile_of(near_ref, far_ref, c, block):
    blocks = near_ref.shape[2] // LANES
    ref = near_ref if block < blocks else far_ref
    at = (block % blocks) * LANES
    return ref[c, :, at : at + LANES]


def first_body(order, low_ref, high_ref, near_ref, far_ref, out_ref):
    blocks, _, rows, depth = low_ref.shape
    span = 2 * LANES
    for p in range(len(order) // 2):
        tiles = [
            jnp.concatenate([tile_of(near_ref, far_ref, c, b) for b in order[2 * p : 2 * p + 2]], axis=1)
            for c in range(2)
        ]
        for at, ref in ((0, low_ref), (blocks * rows, high_ref)):
            left = ref[...].reshape(2 * blocks * rows, depth)
            by_real = jnp.dot(left, tiles[0], preferred_element_type=F32)
            by_imag = jnp.dot(left, tiles[1], preferred_element_type=F32)
            for b in range(blocks):
                real = slice(2 * b * rows, (2 * b + 1) * rows)
                imag = slice((2 * b + 1) * rows, (2 * b + 2) * rows)
                put = (slice(at + b * rows, at + (b + 1) * rows), slice(p * span, (p + 1) * span))
                out_ref[0, put[0], put[1]] = (by_real[real] - by_imag[imag]).astype(out_ref.dtype)
                out_ref[1, put[0], put[1]] = (by_real[imag] + by_imag[real]).astype(out_ref.dtype)


def first_product(line, low, high, near, far, order, kind):
    blocks, _, rows, depth = low.shape
    full = 2 * blocks * rows
    width = len(order) * LANES
    return line.call(
        functools.partial(first_body, order),
        jax.ShapeDtypeStruct((2, full, width), kind),
        [low, high, near, far], [WHOLE] * 4, WHOLE, "first_product", 8, 8 * full * depth * width,
    )


def lane_weights(coupling, shape, axis):
    orbitals = coupling.shape[0]
    at = lax.rem(lax.broadcasted_iota(jnp.int32, shape, axis), orbitals)
    weights = jnp.zeros(shape, F32)
    for a in range(orbitals):
        weights = jnp.where(at == a, coupling[a], weights)
    return weights


def sigma_body(scalars, coupling, strip_ref, own_ref, other_ref):
    _, own_times, orbitals, width = strip_ref.shape
    half = orbitals // 2
    core = scalars[3]
    col = lane_weights(coupling, (1, LANES), 1)
    col = jnp.concatenate([col] * (width // LANES), axis=1)
    row = lane_weights(coupling, (orbitals, LANES), 0)
    row = jnp.concatenate([row] * (width // LANES), axis=1)
    weight = row * col
    for n in range(own_times):
        real = strip_ref[0, n]
        imag = strip_ref[1, n]
        factor = -weight * (real * real + imag * imag)
        for c, part in ((0, real), (1, imag)):
            sigma = part * factor
            first, second = sigma[:half], sigma[half:]
            own = jnp.where(core == 0, first, second)
            other = jnp.where(core == 0, second, first)
            own_ref[c, n] = own.astype(BF16)
            other_ref[c, n] = other.astype(BF16)


def sigma_strip(scalars, coupling, strip):
    _, own_times, orbitals, width = strip.shape
    out = jax.ShapeDtypeStruct((2, own_times, orbitals // 2, width), BF16)
    return pl.pallas_call(
        sigma_body,
        out_shape=[out, out],
        in_specs=[
            pl.BlockSpec(memory_space=pltpu.SMEM),
            pl.BlockSpec(memory_space=pltpu.SMEM),
            pl.BlockSpec(memory_space=pltpu.VMEM),
        ],
        out_specs=[pl.BlockSpec(memory_space=pltpu.VMEM)] * 2,
        compiler_params=pltpu.CompilerParams(vmem_limit_bytes=24 << 20),
        cost_estimate=pl.CostEstimate(flops=3 << 20, bytes_accessed=3 << 20, transcendentals=0),
        name="sigma_strip",
    )(scalars, coupling, strip)


def middle_body(
    first_orbital, scalars, coupling, keep_ref, one_ref, two_ref, three_ref, solve_ref, next_ref, earlier_ref, sigma_ref, turn
):
    rows = three_ref.shape[1]
    times = solve_ref.shape[0] // 2
    count = rows // times
    orbitals = coupling.shape[0]
    for c in range(2):
        total = keep_ref[c, :, :LANES] + one_ref[c, :, :LANES].astype(F32)
        total += two_ref[c, :, :LANES].astype(F32) + three_ref[c].astype(F32)
        turn[c] = TIME_STEP * total

    def column(a):
        return jnp.concatenate([turn[c, pl.ds(a, times, stride=count), :] for c in range(2)], axis=0)

    source = jnp.concatenate([column(a) for a in range(count)], axis=1)
    green = jnp.dot(solve_ref[...], source, precision=HIGHEST, preferred_element_type=F32)
    col = lane_weights(coupling, (1, LANES), 1)
    base = scalars[3] * (orbitals // 2) + first_orbital
    weight = jnp.concatenate([-(coupling[base + a] * col) for a in range(count)], axis=1)
    real = green[:times]
    imag = green[times:]
    factor = weight * (real * real + imag * imag)
    sigma = jnp.concatenate([real * factor, imag * factor], axis=0)
    mixed = jnp.dot(next_ref[...], sigma, precision=HIGHEST, preferred_element_type=F32)
    for value, ref in ((mixed, sigma_ref), (green, earlier_ref)):
        for a in range(count):
            for c in range(2):
                part = value[c * times : (c + 1) * times, a * LANES : (a + 1) * LANES]
                turn[c, pl.ds(a, times, stride=count), :] = part
        for c in range(2):
            ref[0, c] = turn[c].astype(BF16)


def middle(line, first_orbital, scalars, coupling, keep, one, two, three, solve, following):
    rows = three.shape[1]
    share = jax.ShapeDtypeStruct((1, 2, rows, LANES), BF16)
    return line.call(
        functools.partial(middle_body, first_orbital),
        [share, share],
        [scalars, coupling, keep, one, two, three, solve, following],
        [SCALAR, SCALAR] + [WHOLE] * 6, [WHOLE, WHOLE], "middle", 4, 1 << 30,
        scratch=[pltpu.VMEM((2, rows, LANES), F32)],
    )


def second_body(start, order, low_ref, high_ref, near_ref, far_ref, out_ref, left):
    blocks = low_ref.shape[0]
    count = out_ref.shape[1]
    span = blocks * LANES
    tile = 256
    for i, b in enumerate(order):
        ref = low_ref if i < blocks else high_ref
        for c in range(2):
            left[c * count : (c + 1) * count, b * LANES : (b + 1) * LANES] = ref[
                i % blocks, c, start : start + count, :
            ]
    for s in range(out_ref.shape[2] // tile):
        here = slice(s * tile, (s + 1) * tile)

        def by(c):
            return sum(
                lax.dot_general(
                    left[:, at : at + span],
                    ref[c, here],
                    (((1,), (1,)), ((), ())),
                    preferred_element_type=F32,
                )
                for at, ref in ((0, near_ref), (span, far_ref))
            )

        by_real = by(0)
        by_imag = by(1)
        out_ref[0, :, here] = (-(by_real[:count] + by_imag[count:])).astype(out_ref.dtype)
        out_ref[1, :, here] = (by_imag[:count] - by_real[count:]).astype(out_ref.dtype)


def second_product(line, low, high, near, far, order, start, count, kind):
    depth, width = near.shape[1:]
    return line.call(
        functools.partial(second_body, start, order),
        jax.ShapeDtypeStruct((2, count, depth), kind),
        [low, high, near, far], [WHOLE] * 4, WHOLE, "second_product", 8, 16 * count * width * depth,
        scratch=[pltpu.VMEM((2 * count, 2 * width), BF16)],
    )


def split_tiles(line, scalars, near, far):
    out = jax.ShapeDtypeStruct(near.shape, near.dtype)
    return line.call(
        arrange_body, [out, out], [scalars, near, far], [SCALAR, WHOLE, WHOLE], [WHOLE] * 2, "split_tiles", 8, 0
    )


def assemble_body(scalars, mine_ref, others_ref, out_ref):
    times, orbitals = out_ref.shape[1:3]
    width = orbitals // 2
    core = scalars[3]
    per_chunk = width // CHUNKS
    for at, ref in ((core, mine_ref), (1 - core, others_ref)):
        for k in range(CHUNKS):
            for c in range(2):
                value = ref[0, k, c].astype(F32).reshape(times, per_chunk, LANES)
                row = pl.multiple_of(at * width + k * per_chunk, 8)
                out_ref[c, :, pl.ds(row, per_chunk), :] = value


def assemble_earlier(line, scalars, mine, others, times, orbitals):
    blocks = mine.shape[0]
    block = (1,) + mine.shape[1:]
    own = pl.BlockSpec(block, lambda j, s: (s[0] ^ j, 0, 0, 0, 0))
    other = pl.BlockSpec(block, lambda j, s: (s[1] ^ j, 0, 0, 0, 0))
    return line.call(
        assemble_body,
        jax.ShapeDtypeStruct((2, times, orbitals, blocks * LANES), F32),
        [mine, others], [own, other],
        pl.BlockSpec((2, times, orbitals, LANES), lambda j, s: (0, 0, 0, j)),
        "assemble_earlier", 12, 0, grid=(blocks,), scalars=scalars,
    )


def one_hot(position, count):
    return (position[:, None] == jnp.arange(count, dtype=jnp.int32)[None, :]).astype(F32)


def exact_dot(left, right):
    return jnp.dot(left, right, precision=HIGHEST, preferred_element_type=F32)


def later_body(scalars, own_ref, arrived_ref, out_ref):
    half = out_ref.shape[2] // 2
    count = own_ref.shape[3]
    core = scalars[3]
    for at, ref in ((core, own_ref), (1 - core, arrived_ref)):
        for k in range(CHUNKS):
            row = pl.multiple_of(at * half + k * count, 8)
            for c in range(2):
                for n in range(out_ref.shape[1]):
                    out_ref[c, n, pl.ds(row, count), :] = ref[k, c, n]


def assemble_later(line, scalars, own, arrived, orbitals):
    _, _, own_times, count, width = own.shape
    tile = 256
    spec = pl.BlockSpec((CHUNKS, 2, own_times, count, tile), lambda t: (0, 0, 0, 0, t))
    return line.call(
        later_body,
        jax.ShapeDtypeStruct((2, own_times, orbitals, width), F32),
        [scalars, own, arrived], [SCALAR, spec, spec],
        pl.BlockSpec((2, own_times, orbitals, tile), lambda t: (0, 0, 0, t)),
        "assemble_later", 5, 1 << 20, grid=(width // tile,),
    )


def paired(real, imag):
    return jnp.concatenate(
        [jnp.concatenate([real, -imag], axis=1), jnp.concatenate([imag, real], axis=1)], axis=0
    )


def block_order(bits):
    order = [0]
    for bit in bits:
        order += [b + (1 << bit) for b in order]
    return tuple(order)


def shards(history, start_strip, coupling, dyson_inverse):
    orbitals = coupling.shape[0]
    times = dyson_inverse.shape[2]
    yl, x, z, yh, core = [lax.axis_index(a) for a in AXES]
    strip_rows, strip_cols = start_strip.shape[1:]
    own_times = strip_rows // orbitals
    per_chunk = orbitals // 2 // CHUNKS
    chip_times = 2 * own_times
    block_rows = chip_times * per_chunk
    rows = times * per_chunk
    tile_cols = history.shape[2]

    row_place = place_of(yl, x, core)
    other_row_place = place_of(yl, x, 1 - core)
    col_place = place_of(yh, z, core)
    own_near = (row_place >> 2) == core
    scalars = jnp.stack(
        [row_place & 3, other_row_place & 3, own_near.astype(jnp.int32), core]
    ).astype(jnp.int32)

    strip = start_strip.reshape(2, own_times, orbitals, strip_cols)
    sigma_own, sigma_other = sigma_strip(scalars, coupling, strip)
    sigma_core = send(sigma_other, CORE_STEP)
    sigma_next = send(sigma_own, COL_STEPS[0])
    sigma_across = send(sigma_other, COL_ACROSS)
    other_history = send(history, CORE_STEP)
    inner = (jnp.arange(chip_times, dtype=jnp.int32) + own_times * core) % chip_times
    matrices = {}
    for bits in sorted(set(BITS)):
        group = ring_group(col_place ^ jnp.array(block_order(bits), jnp.int32), core)
        order = one_hot((chip_times * group[:, None] + inner[None, :]).reshape(-1), times)
        solve = paired(exact_dot(dyson_inverse[0, 0], order.T), exact_dot(dyson_inverse[0, 1], order.T))
        following = paired(exact_dot(order, dyson_inverse[1, 0]), exact_dot(order, dyson_inverse[1, 1]))
        matrices[bits] = (solve, following)

    line = Line()
    chunks = range(CHUNKS)
    orders = [block_order(bits) for bits in BITS]
    quarter = tile_cols // 4
    parts = (sigma_own, sigma_core, sigma_next, sigma_across)
    low, arriving, high, away, keep, one, two, three = ([None] * CHUNKS for _ in range(8))
    for k in chunks:
        low[k] = as_blocks(line, parts, k, per_chunk)
        arriving[k] = send(low[k], COL_STEPS[BITS[k][1]])
    near, far = arrange_history(line, scalars, history, other_history)
    for k in chunks:
        low[k] = join(line, [low[k], arriving[k]])
        high[k] = send(low[k], COL_STEPS[BITS[k][2]])
    for k in chunks:
        away[k] = first_product(line, low[k], high[k], near, far, orders[k][4:], BF16)
        one[k] = send(away[k], ROW_STEPS[BITS[k][2]])
        keep[k] = first_product(line, low[k], high[k], near, far, orders[k][:4], F32)
    for k in chunks:
        out = fold(line, [keep[k], one[k]], 2, 2 * quarter, 4 * quarter)
        two[k] = send(out, ROW_STEPS[BITS[k][1]])
    for k in chunks:
        out = fold(line, [keep[k], one[k], two[k]], 2, quarter, 2 * quarter)
        three[k] = send(out, ROW_STEPS[BITS[k][0]])
    share, earlier_share = [None] * CHUNKS, [None] * CHUNKS
    for k in chunks:
        earlier_share[k], share[k] = middle(
            line, k * per_chunk, scalars, coupling, keep[k], one[k], two[k], three[k], *matrices[BITS[k]]
        )
        arriving[k] = send(share[k], ROW_STEPS[BITS[k][0]])

    for k in chunks:
        low[k] = join(line, [share[k], arriving[k]])
        arriving[k] = send(low[k], ROW_STEPS[BITS[k][1]])
    for k in chunks:
        low[k] = join(line, [low[k], arriving[k]])
        high[k] = send(low[k], ROW_STEPS[BITS[k][2]])
    for k in chunks:
        away[k] = second_product(line, low[k], high[k], near, far, orders[k], rows // 2, rows // 2, BF16)
        one[k] = send(away[k], COL_STEPS[BITS[k][2]])
        if k == 0:
            earlier = join(line, [e[:, None] for e in earlier_share], axis=1)
            earlier_next = send(earlier, ROW_STEPS[0])
        else:
            earlier = join(line, [earlier, earlier_next])
            earlier_next = send(earlier, ROW_STEPS[1])
        keep[k] = second_product(line, low[k], high[k], near, far, orders[k], 0, rows // 2, F32)
    for k in chunks:
        out = fold(line, [keep[k], one[k]], 1, 2 * block_rows, 4 * block_rows)
        two[k] = send(out, COL_STEPS[BITS[k][1]])
        if k == 1:
            earlier = join(line, [earlier, earlier_next])
            earlier_next = send(earlier, ROW_STEPS[2])
    for k in chunks:
        out = fold(line, [keep[k], one[k], two[k]], 1, block_rows, 2 * block_rows)
        three[k] = send(out, COL_STEPS[BITS[k][0]])
    own, sent = finish(line, [v for k in chunks for v in (keep[k], one[k], two[k], three[k])])
    arrived = send(sent, CORE_STEP)
    split = (CHUNKS, 2, own_times, per_chunk, strip_cols)
    mine, others = split_tiles(line, scalars, earlier, earlier_next)
    others = send(others, CORE_STEP)
    later = assemble_later(line, scalars, own.reshape(split), arrived.reshape(split), orbitals)
    earlier = assemble_earlier(line, scalars, mine, others, times, orbitals)
    return (
        earlier.reshape(2, times * orbitals, tile_cols),
        later.reshape(2, strip_rows, strip_cols),
    )


def solution(mesh):
    finer = Mesh(mesh.devices.reshape(SIZES), AXES)
    in_specs = (P(None, ROW, COL), P(None, COL, ROW), P(), P())
    out_specs = (P(None, None, COL), P(None, COL, ROW))
    return jax.shard_map(
        shards, mesh=finer, in_specs=in_specs, out_specs=out_specs, check_vma=False
    )
```
